32 devices in a mesh: row: 8 (over z, x), layer: 4 (over y, core).
Axes of the slice: x: 2, y: 2, z: 4, core: 2. Of those that a mesh axis runs over, the one named last changes fastest.
Arguments:
- window_points: int32 [2, 8192], P(None, 'row'), may hold values from 0 to 63
- pivot_points: int32 [2, 512], replicated, may hold values from 0 to 63
- window_factor: bfloat16 [8192, 16384], P('row', 'layer'), may hold values from -1.5 to 1.5
- pivot_factor: bfloat16 [512, 16384], P('row', 'layer'), may hold values from -0.0234375 to 0.0234375
- right_sides: bfloat16 [8192, 512], P('row', 'layer'), may hold values from -6 to 6
- pivot_sides: bfloat16 [512, 512], P('row', 'layer'), may hold values from -6 to 6
Outputs:
- panel_factor: float32 [8192, 512], P('row', 'layer')
- eliminated: float32 [8192, 512], P('row', 'layer')
The draws below stay inside these ranges and needn't reach their ends.
All inputs are finite; a program needn't handle non-finite values.
Results may differ from the reference program's by a relative error of at most 0.0006.
Values may be sent and summed in bfloat16 or wider, within the bound.
A program may use at most 64 MiB of HBM per device.

```python
import jax
import jax.numpy as jnp
from jax import lax

K = 16384
P_SIZE = 512
NRHS = 512
GRID = 64
WIN = 8192


def place_ends(array, own_key, smallest, largest):
    dims = array.shape
    spot = [jax.random.randint(jax.random.fold_in(own_key, axis), (), 0, dims[axis]) for axis in range(len(dims))]
    array = array.at[tuple(spot)].set(smallest)
    longest = dims.index(max(dims))
    spot[longest] = (spot[longest] + 1) % dims[longest]
    return array.at[tuple(spot)].set(largest)


def level_of(own_key, shape, cuts, smallest, top_value):
    def one(axis_at, parts):
        heights = jax.random.uniform(jax.random.fold_in(jax.random.fold_in(own_key, 6), axis_at), (parts,), jnp.float32, smallest / len(cuts), top_value / len(cuts))
        return jnp.repeat(jnp.exp(heights), shape[axis_at] // parts).reshape((-1,) + (1,) * (len(shape) - axis_at - 1))

    gain = one(*cuts[0])
    for cut in cuts[1:]:
        gain = gain * one(*cut)
    return gain


def gaussian(rng, extent, deviation, reach, cuts=(), held_as=jnp.bfloat16):
    result = jax.random.normal(rng, extent, jnp.float32) * deviation
    if len(cuts) > 0:
        result = level_of(rng, extent, cuts, -0.22, 0.18) * result
    return jnp.clip(result, min=-reach, max=reach).astype(held_as)


def setup_inputs(seed: int = 0) -> dict:
    key_list = jax.random.split(jax.random.key(seed), 7)
    window_points = place_ends(jax.random.randint(key_list[0], (2, WIN), 0, GRID), jax.random.fold_in(key_list[0], 1), 0, GRID - 1).astype(jnp.int32)
    pivot_points = place_ends(jax.random.randint(key_list[1], (2, P_SIZE), 0, GRID), jax.random.fold_in(key_list[1], 1), 0, GRID - 1).astype(jnp.int32)
    window_factor = gaussian(key_list[2], (WIN, K), (max(K // 1024, 1)) ** -0.5, 1.5, ((0, 8), (1, 4)))
    pivot_factor = gaussian(key_list[3], (P_SIZE, K), (4 * K) ** -0.5, 0.0234375, ((0, 8), (1, 4)))
    right_sides = gaussian(key_list[4], (WIN, NRHS), 1.0, 6.0, ((0, 8), (1, 4)))
    pivot_sides = gaussian(key_list[5], (P_SIZE, NRHS), 1.0, 6.0, ((0, 8), (1, 4)))
    return dict(window_points=window_points, pivot_points=pivot_points, window_factor=window_factor, pivot_factor=pivot_factor, right_sides=right_sides, pivot_sides=pivot_sides)


nugget_value = 2.0
variance_value = 4.0
length_scale = 4.0

def matern(first_points, second_points):
    first_float = first_points.astype(jnp.float32)
    second_float = second_points.astype(jnp.float32)
    delta_x = first_float[0][:, None] - second_float[0][None, :]
    delta_y = first_float[1][:, None] - second_float[1][None, :]
    scaled = jnp.sqrt(delta_x * delta_x + delta_y * delta_y) * (jnp.sqrt(3.0) / length_scale)
    return variance_value * (1.0 + scaled) * jnp.exp(-scaled)

def reference(window_points, pivot_points, window_factor, pivot_factor, right_sides, pivot_sides):
    schur_sum = lax.dot_general(window_factor.astype(jnp.float32), pivot_factor.astype(jnp.float32), (((1,), (1,)), ((), ())), preferred_element_type=jnp.float32)
    gram_sum = lax.dot_general(pivot_factor.astype(jnp.float32), pivot_factor.astype(jnp.float32), (((1,), (1,)), ((), ())), preferred_element_type=jnp.float32)
    count = pivot_points.shape[1]
    diagonal_block = matern(pivot_points, pivot_points) + nugget_value * jnp.eye(count, dtype=jnp.float32) - gram_sum
    factor = jnp.linalg.cholesky(diagonal_block)
    panel_block = matern(window_points, pivot_points) - schur_sum
    solved = jax.scipy.linalg.solve_triangular(factor, panel_block.T, lower=True).T
    reduced = jax.scipy.linalg.solve_triangular(factor, pivot_sides.astype(jnp.float32), lower=True)
    eliminated = right_sides.astype(jnp.float32) - jnp.dot(solved, reduced, precision=lax.Precision.HIGHEST)
    return (solved, eliminated)
```

```python
import jax
import jax.numpy as jnp
from jax import lax
from jax.experimental import pallas as pl
from jax.experimental.pallas import tpu as pltpu
from jax.sharding import PartitionSpec as P

nugget_value = 2.0
variance_value = 4.0
length_scale = 4.0


def matern(first_points, second_points):
    first_float = first_points.astype(jnp.float32)
    second_float = second_points.astype(jnp.float32)
    delta_x = first_float[0][:, None] - second_float[0][None, :]
    delta_y = first_float[1][:, None] - second_float[1][None, :]
    scaled = jnp.sqrt(delta_x * delta_x + delta_y * delta_y) * (jnp.sqrt(3.0) / length_scale)
    return variance_value * (1.0 + scaled) * jnp.exp(-scaled)


lanes = 128
tile_rows = 8
group = 4
highest = lax.Precision.HIGHEST


def invert_tile(read_tile, write_row):
    shape = (tile_rows, lanes)
    count = lanes // tile_rows
    row_of = lax.broadcasted_iota(jnp.int32, shape, 0)
    lane_of = lax.broadcasted_iota(jnp.int32, shape, 1)
    block = [read_tile(t) for t in range(count)]
    extra = [jnp.where(row_of + t * tile_rows == lane_of, 1.0, 0.0) for t in range(count)]
    for first in range(0, lanes, group):
        top, low = first // tile_rows, first % tile_rows
        live = range(top, count)
        columns = [
            {t: jnp.broadcast_to(block[t][:, first + k : first + k + 1], shape) for t in live}
            for k in range(group)
        ]

        def spread(tile, k):
            return jnp.broadcast_to(tile[low + k : low + k + 1, :], shape)

        rows = [spread(block[top], k) for k in range(group)]
        ends = [spread(extra[top], k) for k in range(group)]
        for k in range(group):
            pivot = spread(columns[k][top], k)
            inverse = 1.0 / pivot
            write_row(first + k, (ends[k] * lax.rsqrt(pivot))[0:1, :])
            for m in range(k + 1, group):
                factor = spread(columns[k][top], m) * inverse
                rows[m] = rows[m] - factor * rows[k]
                ends[m] = ends[m] - factor * ends[k]
                for t in live:
                    columns[m][t] = columns[m][t] - columns[k][t] * factor
            rows[k] = rows[k] * inverse
            ends[k] = ends[k] * inverse
        for t in live:
            if t == top and low + group == tile_rows:
                continue
            for k in range(group):
                weight = columns[k][t]
                if t == top:
                    weight = jnp.where(row_of >= low + group, weight, 0.0)
                block[t] = block[t] - weight * rows[k]
                extra[t] = extra[t] - weight * ends[k]


def inverse_kernel(matrix_ref, out_ref, work_ref, tile_ref):
    size = matrix_ref.shape[0]
    work_ref[:, :size] = matrix_ref[...]
    row_of = lax.broadcasted_iota(jnp.int32, (size, size), 0)
    lane_of = lax.broadcasted_iota(jnp.int32, (size, size), 1)
    work_ref[:, size:] = jnp.where(row_of == lane_of, 1.0, 0.0)

    def step(index, carry):
        start = pl.multiple_of(index * lanes, lanes)

        def read_tile(t):
            return work_ref[pl.ds(start + t * tile_rows, tile_rows), pl.ds(start, lanes)]

        def write_row(at, value):
            tile_ref[at : at + 1, :] = value

        invert_tile(read_tile, write_row)
        solved = jnp.dot(
            tile_ref[...],
            work_ref[pl.ds(start, lanes), :],
            precision=highest,
            preferred_element_type=jnp.float32,
        )
        out_ref[pl.ds(start, lanes), :] = solved[:, size:]
        below = lax.broadcasted_iota(jnp.int32, (lanes, size), 1) >= start + lanes
        left = jnp.where(below, solved[:, :size], 0.0)
        work_ref[...] -= jnp.dot(
            left.T, solved, precision=highest, preferred_element_type=jnp.float32
        )
        return carry

    lax.fori_loop(0, size // lanes, step, 0)


def inverse_factor(matrix):
    size = matrix.shape[0]
    return pl.pallas_call(
        inverse_kernel,
        out_shape=jax.ShapeDtypeStruct((size, size), jnp.float32),
        in_specs=[pl.BlockSpec(memory_space=pltpu.VMEM)],
        out_specs=pl.BlockSpec(memory_space=pltpu.VMEM),
        scratch_shapes=[
            pltpu.VMEM((size, 2 * size), jnp.float32),
            pltpu.VMEM((lanes, lanes), jnp.float32),
        ],
        compiler_params=pltpu.CompilerParams(vmem_limit_bytes=32 * 1024 * 1024),
    )(matrix)


def shards(window_points, pivot_points, window_factor, pivot_factor, right_sides, pivot_sides):
    pivots, pivot_block = (
        lax.all_gather(pivot_factor, "row", axis=0, tiled=True),
        lax.all_gather(pivot_sides, "row", axis=0, tiled=True),
    )
    contract = (((1,), (1,)), ((), ()))
    partial_value = lax.dot_general(
        window_factor, pivots, contract, preferred_element_type=jnp.float32
    )
    gram_part = lax.dot_general(pivots, pivots, contract, preferred_element_type=jnp.float32)
    count = pivots.shape[0]
    cov_diagonal = matern(pivot_points, pivot_points) + nugget_value * jnp.eye(
        count, dtype=jnp.float32
    )
    layers = lax.axis_size("layer")
    layer_index = lax.axis_index("layer")
    rows_here = window_factor.shape[0] // layers
    own_points = lax.dynamic_slice_in_dim(window_points, layer_index * rows_here, rows_here, 1)
    cov_rows = matern(own_points, pivot_points)
    schur_part = lax.psum_scatter(partial_value, "layer", scatter_dimension=0, tiled=True)
    gram_sum = lax.psum(gram_part.astype(jnp.bfloat16), "layer").astype(jnp.float32)
    all_sides = lax.all_gather(pivot_block, "layer", axis=1, tiled=True)
    inverse = inverse_factor(cov_diagonal - gram_sum)
    solved_rows = lax.dot_general(
        cov_rows - schur_part, inverse, contract, precision=highest
    )
    reduced = jnp.dot(inverse, all_sides.astype(jnp.float32), precision=highest)
    update_rows = jnp.dot(solved_rows, reduced, precision=highest)
    both = jnp.stack([solved_rows, update_rows])
    moved = lax.all_to_all(both, "layer", split_axis=2, concat_axis=1, tiled=True)
    panel_out, update = moved[0], moved[1]
    eliminated = right_sides.astype(jnp.float32) - update
    return (panel_out, eliminated)


def solution(mesh):
    placed = (
        P(None, "row"),
        P(),
        P("row", "layer"),
        P("row", "layer"),
        P("row", "layer"),
        P("row", "layer"),
    )
    return jax.shard_map(
        shards,
        mesh=mesh,
        in_specs=placed,
        out_specs=(P("row", "layer"), P("row", "layer")),
        check_vma=False,
    )
```

```python
import functools

import jax
import jax.numpy as jnp
from jax import lax
from jax.experimental import pallas as pl
from jax.experimental.pallas import tpu as pltpu
from jax.sharding import PartitionSpec as P

nugget_value = 2.0
variance_value = 4.0
length_scale = 4.0


def matern(first_points, second_points):
    first_float = first_points.astype(jnp.float32)
    second_float = second_points.astype(jnp.float32)
    delta_x = first_float[0][:, None] - second_float[0][None, :]
    delta_y = first_float[1][:, None] - second_float[1][None, :]
    scaled = jnp.sqrt(delta_x * delta_x + delta_y * delta_y) * (jnp.sqrt(3.0) / length_scale)
    return variance_value * (1.0 + scaled) * jnp.exp(-scaled)


lanes = 128
tile_rows = 8
group = 4
highest = lax.Precision.HIGHEST


def invert_tile(read_tile, write_row):
    shape = (tile_rows, lanes)
    count = lanes // tile_rows
    row_of = lax.broadcasted_iota(jnp.int32, shape, 0)
    lane_of = lax.broadcasted_iota(jnp.int32, shape, 1)
    block = [read_tile(t) for t in range(count)]
    extra = [jnp.where(row_of + t * tile_rows == lane_of, 1.0, 0.0) for t in range(count)]
    for first in range(0, lanes, group):
        top, low = first // tile_rows, first % tile_rows
        live = range(top, count)
        columns = [
            {t: jnp.broadcast_to(block[t][:, first + k : first + k + 1], shape) for t in live}
            for k in range(group)
        ]

        def spread(tile, k):
            return jnp.broadcast_to(tile[low + k : low + k + 1, :], shape)

        rows = [spread(block[top], k) for k in range(group)]
        ends = [spread(extra[top], k) for k in range(group)]
        for k in range(group):
            pivot = spread(columns[k][top], k)
            inverse = 1.0 / pivot
            write_row(first + k, (ends[k] * lax.rsqrt(pivot))[0:1, :])
            for m in range(k + 1, group):
                factor = spread(columns[k][top], m) * inverse
                rows[m] = rows[m] - factor * rows[k]
                ends[m] = ends[m] - factor * ends[k]
                for t in live:
                    columns[m][t] = columns[m][t] - columns[k][t] * factor
            rows[k] = rows[k] * inverse
            ends[k] = ends[k] * inverse
        for t in live:
            if t == top and low + group == tile_rows:
                continue
            for k in range(group):
                weight = columns[k][t]
                if t == top:
                    weight = jnp.where(row_of >= low + group, weight, 0.0)
                block[t] = block[t] - weight * rows[k]
                extra[t] = extra[t] - weight * ends[k]


def inverse_kernel(matrix_ref, out_ref, work_ref, tile_ref):
    size = matrix_ref.shape[0]
    work_ref[:, :size] = matrix_ref[...]
    row_of = lax.broadcasted_iota(jnp.int32, (size, size), 0)
    lane_of = lax.broadcasted_iota(jnp.int32, (size, size), 1)
    work_ref[:, size:] = jnp.where(row_of == lane_of, 1.0, 0.0)

    def step(index, carry):
        start = pl.multiple_of(index * lanes, lanes)

        def read_tile(t):
            return work_ref[pl.ds(start + t * tile_rows, tile_rows), pl.ds(start, lanes)]

        def write_row(at, value):
            tile_ref[at : at + 1, :] = value

        invert_tile(read_tile, write_row)
        solved = jnp.dot(
            tile_ref[...],
            work_ref[pl.ds(start, lanes), :],
            precision=highest,
            preferred_element_type=jnp.float32,
        )
        out_ref[pl.ds(start, lanes), :] = solved[:, size:]
        below = lax.broadcasted_iota(jnp.int32, (lanes, size), 1) >= start + lanes
        left = jnp.where(below, solved[:, :size], 0.0)
        work_ref[...] -= jnp.dot(
            left.T, solved, precision=highest, preferred_element_type=jnp.float32
        )
        return carry

    lax.fori_loop(0, size // lanes, step, 0)


def inverse_factor(matrix):
    size = matrix.shape[0]
    return pl.pallas_call(
        inverse_kernel,
        out_shape=jax.ShapeDtypeStruct((size, size), jnp.float32),
        in_specs=[pl.BlockSpec(memory_space=pltpu.VMEM)],
        out_specs=pl.BlockSpec(memory_space=pltpu.VMEM),
        scratch_shapes=[
            pltpu.VMEM((size, 2 * size), jnp.float32),
            pltpu.VMEM((lanes, lanes), jnp.float32),
        ],
        compiler_params=pltpu.CompilerParams(vmem_limit_bytes=32 * 1024 * 1024),
    )(matrix)


def remote(src, dst, send, recv, axis, target):
    return pltpu.make_async_remote_copy(
        src_ref=src,
        dst_ref=dst,
        send_sem=send,
        recv_sem=recv,
        device_id={axis: target},
        device_id_type=pl.DeviceIdType.MESH,
    )


def greet(axis, targets):
    barrier = pltpu.get_barrier_semaphore()
    for target in targets:
        pl.semaphore_signal(
            barrier, inc=1, device_id={axis: target}, device_id_type=pl.DeviceIdType.MESH
        )
    pl.semaphore_wait(barrier, len(targets))


def gather_kernel(axis, count, split, block_ref, out_ref, send_sem, recv_sem):
    me = lax.axis_index(axis)
    odd = me % 2
    place = (1 - odd) * (me // 2) + odd * (count - 1 - me // 2)

    def member(spot):
        spot = (spot + count) % count
        upper = spot // (count // 2)
        return (1 - upper) * (2 * spot) + upper * (2 * (count - 1 - spot) + 1)

    right, left = member(place + 1), member(place - 1)
    greet(axis, (left, right))
    copies = []
    for step in range(count - 1):
        for way, target, part in ((0, right, pl.ds(0, split)), (1, left, pl.ds(split, block_ref.shape[1] - split))):
            owner = member(place - step) if way == 0 else member(place + step)
            source = block_ref.at[:, part] if step == 0 else out_ref.at[owner, :, part]
            copy = remote(
                source,
                out_ref.at[owner, :, part],
                send_sem.at[way, step],
                recv_sem.at[way, step],
                axis,
                target,
            )
            if step > 0:
                copies[2 * (step - 1) + way].wait_recv()
            copy.start()
            copies.append(copy)
        if step == 0:
            out_ref[me] = block_ref[...]
    for copy in copies[-2:]:
        copy.wait_recv()
    for copy in copies:
        copy.wait_send()


def gather_rows(block, axis):
    count = lax.axis_size(axis)
    rows, columns = block.shape
    split = columns // 256 * 128
    vmem = pl.BlockSpec(memory_space=pltpu.VMEM)
    return pl.pallas_call(
        functools.partial(gather_kernel, axis, count, split),
        out_shape=jax.ShapeDtypeStruct((count, rows, columns), block.dtype),
        in_specs=[vmem],
        out_specs=vmem,
        scratch_shapes=[
            pltpu.SemaphoreType.DMA((2, count - 1)),
            pltpu.SemaphoreType.DMA((2, count - 1)),
        ],
        compiler_params=pltpu.CompilerParams(
            collective_id=0, has_side_effects=True, vmem_limit_bytes=32 * 1024 * 1024
        ),
    )(block)


def sum_kernel(axis, count, part_ref, sides_ref, total_ref, all_ref, out_buf, in_buf, send_sem, recv_sem):
    me = lax.axis_index(axis)
    rounds = count.bit_length() - 1
    greet(axis, [(me + shift) % count for shift in range(1, count)])
    copies = []
    for level in range(rounds):
        bit = 1 << level
        partner = me + (1 - 2 * ((me // bit) % 2)) * bit
        source = part_ref if level == 0 else out_buf.at[level]
        copy = remote(
            source, in_buf.at[level], send_sem.at[level], recv_sem.at[level], axis, partner
        )
        copy.start()
        if level == 0:
            for shift in range(1, count):
                spot = rounds + shift - 1
                copies.append(
                    remote(
                        sides_ref,
                        all_ref.at[me],
                        send_sem.at[spot],
                        recv_sem.at[spot],
                        axis,
                        (me + shift) % count,
                    )
                )
                copies[-1].start()
            all_ref[me] = sides_ref[...]
        copy.wait()
        total = source[...].astype(jnp.float32) + in_buf[level].astype(jnp.float32)
        if level + 1 < rounds:
            out_buf[level + 1] = total.astype(out_buf.dtype)
        else:
            total_ref[...] = total
    for copy in copies:
        copy.wait()


def sum_parts(part, sides, axis):
    count = lax.axis_size(axis)
    rounds = count.bit_length() - 1
    copies = rounds + count - 1
    vmem = pl.BlockSpec(memory_space=pltpu.VMEM)
    return pl.pallas_call(
        functools.partial(sum_kernel, axis, count),
        out_shape=(
            jax.ShapeDtypeStruct(part.shape, jnp.float32),
            jax.ShapeDtypeStruct((count,) + sides.shape, sides.dtype),
        ),
        in_specs=[vmem, vmem],
        out_specs=(vmem, vmem),
        scratch_shapes=[
            pltpu.VMEM((rounds,) + part.shape, part.dtype),
            pltpu.VMEM((rounds,) + part.shape, part.dtype),
            pltpu.SemaphoreType.DMA((copies,)),
            pltpu.SemaphoreType.DMA((copies,)),
        ],
        compiler_params=pltpu.CompilerParams(
            collective_id=1, has_side_effects=True, vmem_limit_bytes=32 * 1024 * 1024
        ),
    )(part, sides)


def shards(window_points, pivot_points, window_factor, pivot_factor, right_sides, pivot_sides):
    depth, width = pivot_factor.shape[1], pivot_sides.shape[1]
    padded = jnp.pad(pivot_sides, ((0, 0), (0, -width % lanes)))
    gathered = gather_rows(jnp.concatenate([pivot_factor, padded], axis=1), "row")
    gathered = gathered.reshape(-1, gathered.shape[2])
    pivots, pivot_block = gathered[:, :depth], gathered[:, depth : depth + width]
    contract = (((1,), (1,)), ((), ()))
    partial_value = lax.dot_general(
        window_factor, pivots, contract, preferred_element_type=jnp.float32
    )
    gram_part = lax.dot_general(pivots, pivots, contract, preferred_element_type=jnp.float32)
    count = pivots.shape[0]
    cov_diagonal = matern(pivot_points, pivot_points) + nugget_value * jnp.eye(
        count, dtype=jnp.float32
    )
    layers = lax.axis_size("layer")
    layer_index = lax.axis_index("layer")
    rows_here = window_factor.shape[0] // layers
    own_points = lax.dynamic_slice_in_dim(window_points, layer_index * rows_here, rows_here, 1)
    cov_rows = matern(own_points, pivot_points)
    schur_part = lax.psum_scatter(partial_value, "layer", scatter_dimension=0, tiled=True)
    gram_sum, all_parts = sum_parts(gram_part.astype(jnp.bfloat16), pivot_block, "layer")
    all_sides = jnp.swapaxes(all_parts, 0, 1).reshape(count, layers * width)
    inverse = inverse_factor(cov_diagonal - gram_sum)
    solved_rows = lax.dot_general(
        cov_rows - schur_part, inverse, contract, precision=highest
    )
    reduced = jnp.dot(inverse, all_sides.astype(jnp.float32), precision=highest)
    update_rows = jnp.dot(solved_rows, reduced, precision=highest)
    both = jnp.stack([solved_rows, update_rows])
    moved = lax.all_to_all(both, "layer", split_axis=2, concat_axis=1, tiled=True)
    panel_out, update = moved[0], moved[1]
    eliminated = right_sides.astype(jnp.float32) - update
    return (panel_out, eliminated)


def solution(mesh):
    placed = (
        P(None, "row"),
        P(),
        P("row", "layer"),
        P("row", "layer"),
        P("row", "layer"),
        P("row", "layer"),
    )
    return jax.shard_map(
        shards,
        mesh=mesh,
        in_specs=placed,
        out_specs=(P("row", "layer"), P("row", "layer")),
        check_vma=False,
    )
```

```python
import functools

import jax
import jax.numpy as jnp
from jax import lax
from jax.experimental import pallas as pl
from jax.experimental.pallas import tpu as pltpu
from jax.sharding import PartitionSpec as P

nugget_value = 2.0
variance_value = 4.0
length_scale = 4.0


def matern(first_points, second_points):
    first_float = first_points.astype(jnp.float32)
    second_float = second_points.astype(jnp.float32)
    delta_x = first_float[0][:, None] - second_float[0][None, :]
    delta_y = first_float[1][:, None] - second_float[1][None, :]
    scaled = jnp.sqrt(delta_x * delta_x + delta_y * delta_y) * (jnp.sqrt(3.0) / length_scale)
    return variance_value * (1.0 + scaled) * jnp.exp(-scaled)


lanes = 128
tile_rows = 8
group = 4
ring_parts = 4
highest = lax.Precision.HIGHEST


def invert_tile(read_tile, write_row):
    shape = (tile_rows, lanes)
    count = lanes // tile_rows
    row_of = lax.broadcasted_iota(jnp.int32, shape, 0)
    lane_of = lax.broadcasted_iota(jnp.int32, shape, 1)
    block = [read_tile(t) for t in range(count)]
    extra = [jnp.where(row_of + t * tile_rows == lane_of, 1.0, 0.0) for t in range(count)]
    for first in range(0, lanes, group):
        top, low = first // tile_rows, first % tile_rows
        live = range(top, count)
        columns = [
            {t: jnp.broadcast_to(block[t][:, first + k : first + k + 1], shape) for t in live}
            for k in range(group)
        ]

        def spread(tile, k):
            return jnp.broadcast_to(tile[low + k : low + k + 1, :], shape)

        rows = [spread(block[top], k) for k in range(group)]
        ends = [spread(extra[top], k) for k in range(group)]
        for k in range(group):
            pivot = spread(columns[k][top], k)
            inverse = 1.0 / pivot
            write_row(first + k, (ends[k] * lax.rsqrt(pivot))[0:1, :])
            for m in range(k + 1, group):
                factor = spread(columns[k][top], m) * inverse
                rows[m] = rows[m] - factor * rows[k]
                ends[m] = ends[m] - factor * ends[k]
                for t in live:
                    columns[m][t] = columns[m][t] - columns[k][t] * factor
            rows[k] = rows[k] * inverse
            ends[k] = ends[k] * inverse
        for t in live:
            if t == top and low + group == tile_rows:
                continue
            for k in range(group):
                weight = columns[k][t]
                if t == top:
                    weight = jnp.where(row_of >= low + group, weight, 0.0)
                block[t] = block[t] - weight * rows[k]
                extra[t] = extra[t] - weight * ends[k]


def inverse_kernel(matrix_ref, out_ref, work_ref, tile_ref):
    size = matrix_ref.shape[0]
    work_ref[:, :size] = matrix_ref[...]
    row_of = lax.broadcasted_iota(jnp.int32, (size, size), 0)
    lane_of = lax.broadcasted_iota(jnp.int32, (size, size), 1)
    work_ref[:, size:] = jnp.where(row_of == lane_of, 1.0, 0.0)

    def step(index, carry):
        start = pl.multiple_of(index * lanes, lanes)

        def read_tile(t):
            return work_ref[pl.ds(start + t * tile_rows, tile_rows), pl.ds(start, lanes)]

        def write_row(at, value):
            tile_ref[at : at + 1, :] = value

        invert_tile(read_tile, write_row)
        solved = jnp.dot(
            tile_ref[...],
            work_ref[pl.ds(start, lanes), :],
            precision=highest,
            preferred_element_type=jnp.float32,
        )
        out_ref[pl.ds(start, lanes), :] = solved[:, size:]
        below = lax.broadcasted_iota(jnp.int32, (lanes, size), 1) >= start + lanes
        left = jnp.where(below, solved[:, :size], 0.0)
        work_ref[...] -= jnp.dot(
            left.T, solved, precision=highest, preferred_element_type=jnp.float32
        )
        return carry

    lax.fori_loop(0, size // lanes, step, 0)


def inverse_factor(matrix):
    size = matrix.shape[0]
    return pl.pallas_call(
        inverse_kernel,
        out_shape=jax.ShapeDtypeStruct((size, size), jnp.float32),
        in_specs=[pl.BlockSpec(memory_space=pltpu.VMEM)],
        out_specs=pl.BlockSpec(memory_space=pltpu.VMEM),
        scratch_shapes=[
            pltpu.VMEM((size, 2 * size), jnp.float32),
            pltpu.VMEM((lanes, lanes), jnp.float32),
        ],
        compiler_params=pltpu.CompilerParams(vmem_limit_bytes=32 * 1024 * 1024),
    )(matrix)


def remote(src, dst, send, recv, axis, target):
    return pltpu.make_async_remote_copy(
        src_ref=src,
        dst_ref=dst,
        send_sem=send,
        recv_sem=recv,
        device_id={axis: target},
        device_id_type=pl.DeviceIdType.MESH,
    )


def greet(axis, targets):
    barrier = pltpu.get_barrier_semaphore()
    for target in targets:
        pl.semaphore_signal(
            barrier, inc=1, device_id={axis: target}, device_id_type=pl.DeviceIdType.MESH
        )
    pl.semaphore_wait(barrier, len(targets))


def gather_kernel(axis, count, parts, block_ref, out_ref, send_sem, recv_sem):
    me = lax.axis_index(axis)
    odd = me % 2
    place = (1 - odd) * (me // 2) + odd * (count - 1 - me // 2)

    def member(spot):
        spot = (spot + count) % count
        upper = spot // (count // 2)
        return (1 - upper) * (2 * spot) + upper * (2 * (count - 1 - spot) + 1)

    right, left = member(place + 1), member(place - 1)
    greet(axis, (left, right))
    copies = []
    for step in range(count - 1):
        for lane, (start, stop) in enumerate(parts):
            way = lane % 2
            part = pl.ds(start, stop - start)
            owner = member(place - step) if way == 0 else member(place + step)
            source = block_ref.at[:, part] if step == 0 else out_ref.at[owner, :, part]
            copy = remote(
                source,
                out_ref.at[owner, :, part],
                send_sem.at[lane, step],
                recv_sem.at[lane, step],
                axis,
                right if way == 0 else left,
            )
            if step > 0:
                copies[len(parts) * (step - 1) + lane].wait_recv()
            copy.start()
            copies.append(copy)
        if step == 0:
            out_ref[me] = block_ref[...]
    for copy in copies[-len(parts) :]:
        copy.wait_recv()
    for copy in copies:
        copy.wait_send()


def gather_rows(block, axis):
    count = lax.axis_size(axis)
    rows, columns = block.shape
    pieces = columns // lanes
    cuts = [pieces * at // ring_parts * lanes for at in range(ring_parts)] + [columns]
    parts = tuple(zip(cuts[:-1], cuts[1:]))
    vmem = pl.BlockSpec(memory_space=pltpu.VMEM)
    return pl.pallas_call(
        functools.partial(gather_kernel, axis, count, parts),
        out_shape=jax.ShapeDtypeStruct((count, rows, columns), block.dtype),
        in_specs=[vmem],
        out_specs=vmem,
        scratch_shapes=[
            pltpu.SemaphoreType.DMA((ring_parts, count - 1)),
            pltpu.SemaphoreType.DMA((ring_parts, count - 1)),
        ],
        compiler_params=pltpu.CompilerParams(
            collective_id=0, has_side_effects=True, vmem_limit_bytes=32 * 1024 * 1024
        ),
    )(block)


def sum_kernel(axis, count, part_ref, sides_ref, total_ref, all_ref, out_buf, in_buf, send_sem, recv_sem):
    me = lax.axis_index(axis)
    rounds = count.bit_length() - 1
    greet(axis, [(me + shift) % count for shift in range(1, count)])
    copies = []
    for level in range(rounds):
        bit = 1 << level
        partner = me + (1 - 2 * ((me // bit) % 2)) * bit
        source = part_ref if level == 0 else out_buf.at[level]
        copy = remote(
            source, in_buf.at[level], send_sem.at[level], recv_sem.at[level], axis, partner
        )
        copy.start()
        if level == 0:
            for shift in range(1, count):
                spot = rounds + shift - 1
                copies.append(
                    remote(
                        sides_ref,
                        all_ref.at[me],
                        send_sem.at[spot],
                        recv_sem.at[spot],
                        axis,
                        (me + shift) % count,
                    )
                )
                copies[-1].start()
            all_ref[me] = sides_ref[...]
        copy.wait()
        total = source[...].astype(jnp.float32) + in_buf[level].astype(jnp.float32)
        if level + 1 < rounds:
            out_buf[level + 1] = total.astype(out_buf.dtype)
        else:
            total_ref[...] = total
    for copy in copies:
        copy.wait()


def sum_parts(part, sides, axis):
    count = lax.axis_size(axis)
    rounds = count.bit_length() - 1
    copies = rounds + count - 1
    vmem = pl.BlockSpec(memory_space=pltpu.VMEM)
    return pl.pallas_call(
        functools.partial(sum_kernel, axis, count),
        out_shape=(
            jax.ShapeDtypeStruct(part.shape, jnp.float32),
            jax.ShapeDtypeStruct((count,) + sides.shape, sides.dtype),
        ),
        in_specs=[vmem, vmem],
        out_specs=(vmem, vmem),
        scratch_shapes=[
            pltpu.VMEM((rounds,) + part.shape, part.dtype),
            pltpu.VMEM((rounds,) + part.shape, part.dtype),
            pltpu.SemaphoreType.DMA((copies,)),
            pltpu.SemaphoreType.DMA((copies,)),
        ],
        compiler_params=pltpu.CompilerParams(
            collective_id=1, has_side_effects=True, vmem_limit_bytes=32 * 1024 * 1024
        ),
    )(part, sides)


def finish_kernel(
    axis, count, rows_ref, inverse_ref, reduced_ref, right_ref, panel_ref, rest_ref,
    panel_buf, update_buf, land_buf, send_sem, recv_sem
):
    me = lax.axis_index(axis)
    width = panel_ref.shape[2]
    greet(axis, [(me + shift) % count for shift in range(1, count)])
    copies = []

    def send(kind, source, target_ref):
        for shift in range(1, count):
            target = (me + shift) % count
            copy = remote(
                source.at[target],
                target_ref.at[me],
                send_sem.at[kind, shift - 1],
                recv_sem.at[kind, shift - 1],
                axis,
                target,
            )
            copy.start()
            copies.append(copy)
        target_ref[me] = source[me]

    solved = lax.dot_general(
        rows_ref[...],
        inverse_ref[...],
        (((1,), (1,)), ((), ())),
        precision=highest,
        preferred_element_type=jnp.float32,
    )
    for part in range(count):
        panel_buf[part] = solved[:, part * width : (part + 1) * width]
    send(0, panel_buf, panel_ref)
    update = jnp.dot(
        solved, reduced_ref[...], precision=highest, preferred_element_type=jnp.float32
    )
    for part in range(count):
        update_buf[part] = update[:, part * width : (part + 1) * width]
    send(1, update_buf, land_buf)
    for copy in copies:
        copy.wait()
    rest_ref[...] = right_ref[...].astype(jnp.float32) - land_buf[...]


def finish(rows, inverse, reduced, right, axis):
    count = lax.axis_size(axis)
    shape = (count, rows.shape[0], right.shape[1])
    vmem = pl.BlockSpec(memory_space=pltpu.VMEM)
    out = jax.ShapeDtypeStruct(shape, jnp.float32)
    panel, rest = pl.pallas_call(
        functools.partial(finish_kernel, axis, count),
        out_shape=(out, out),
        in_specs=[vmem] * 4,
        out_specs=(vmem, vmem),
        scratch_shapes=[pltpu.VMEM(shape, jnp.float32)] * 3
        + [pltpu.SemaphoreType.DMA((2, count - 1))] * 2,
        compiler_params=pltpu.CompilerParams(
            collective_id=2, has_side_effects=True, vmem_limit_bytes=32 * 1024 * 1024
        ),
    )(rows, inverse, reduced, right.reshape(shape))
    return panel.reshape(right.shape), rest.reshape(right.shape)


def shards(window_points, pivot_points, window_factor, pivot_factor, right_sides, pivot_sides):
    depth, width = pivot_factor.shape[1], pivot_sides.shape[1]
    padded = jnp.pad(pivot_sides, ((0, 0), (0, -width % lanes)))
    gathered = gather_rows(jnp.concatenate([pivot_factor, padded], axis=1), "row")
    gathered = gathered.reshape(-1, gathered.shape[2])
    pivots, pivot_block = gathered[:, :depth], gathered[:, depth : depth + width]
    contract = (((1,), (1,)), ((), ()))
    gram_part = lax.dot_general(pivots, pivots, contract, preferred_element_type=jnp.float32)
    count = pivots.shape[0]
    cov_diagonal = matern(pivot_points, pivot_points) + nugget_value * jnp.eye(
        count, dtype=jnp.float32
    )
    layers = lax.axis_size("layer")
    layer_index = lax.axis_index("layer")
    rows_here = window_factor.shape[0] // layers
    own_points = lax.dynamic_slice_in_dim(window_points, layer_index * rows_here, rows_here, 1)
    cov_rows = matern(own_points, pivot_points)
    gram_sum, all_parts = sum_parts(gram_part.astype(jnp.bfloat16), pivot_block, "layer")
    gathered, gram_sum = lax.optimization_barrier((gathered, gram_sum))
    partial_value = lax.dot_general(
        window_factor, gathered[:, :depth], contract, preferred_element_type=jnp.float32
    )
    schur_part = lax.psum_scatter(partial_value, "layer", scatter_dimension=0, tiled=True)
    all_sides = jnp.swapaxes(all_parts, 0, 1).reshape(count, layers * width)
    inverse = inverse_factor(cov_diagonal - gram_sum)
    reduced = jnp.dot(inverse, all_sides.astype(jnp.float32), precision=highest)
    return finish(cov_rows - schur_part, inverse, reduced, right_sides, "layer")


def solution(mesh):
    placed = (
        P(None, "row"),
        P(),
        P("row", "layer"),
        P("row", "layer"),
        P("row", "layer"),
        P("row", "layer"),
    )
    return jax.shard_map(
        shards,
        mesh=mesh,
        in_specs=placed,
        out_specs=(P("row", "layer"), P("row", "layer")),
        check_vma=False,
    )
```

```python
import functools

import jax
import jax.numpy as jnp
from jax import lax
from jax.experimental import pallas as pl
from jax.experimental.pallas import tpu as pltpu
from jax.sharding import PartitionSpec as P

nugget_value = 2.0
variance_value = 4.0
length_scale = 4.0


def matern(first_points, second_points):
    first_float = first_points.astype(jnp.float32)
    second_float = second_points.astype(jnp.float32)
    delta_x = first_float[0][:, None] - second_float[0][None, :]
    delta_y = first_float[1][:, None] - second_float[1][None, :]
    scaled = jnp.sqrt(delta_x * delta_x + delta_y * delta_y) * (jnp.sqrt(3.0) / length_scale)
    return variance_value * (1.0 + scaled) * jnp.exp(-scaled)


lanes = 128
tile_rows = 8
group = 8
ring_parts = 4
highest = lax.Precision.HIGHEST


def invert_tile(read_tile, write_row):
    shape = (tile_rows, lanes)
    count = lanes // tile_rows
    row_of = lax.broadcasted_iota(jnp.int32, shape, 0)
    lane_of = lax.broadcasted_iota(jnp.int32, shape, 1)
    block = [read_tile(t) for t in range(count)]
    extra = [jnp.where(row_of + t * tile_rows == lane_of, 1.0, 0.0) for t in range(count)]
    for first in range(0, lanes, group):
        top, low = first // tile_rows, first % tile_rows
        live = range(top, count)
        columns = [
            {t: jnp.broadcast_to(block[t][:, first + k : first + k + 1], shape) for t in live}
            for k in range(group)
        ]

        def spread(tile, k):
            return jnp.broadcast_to(tile[low + k : low + k + 1, :], shape)

        rows = [spread(block[top], k) for k in range(group)]
        ends = [spread(extra[top], k) for k in range(group)]
        for k in range(group):
            pivot = spread(columns[k][top], k)
            inverse = 1.0 / pivot
            write_row(first + k, (ends[k] * lax.rsqrt(pivot))[0:1, :])
            for m in range(k + 1, group):
                factor = spread(columns[k][top], m) * inverse
                rows[m] = rows[m] - factor * rows[k]
                ends[m] = ends[m] - factor * ends[k]
                for t in live:
                    columns[m][t] = columns[m][t] - columns[k][t] * factor
            rows[k] = rows[k] * inverse
            ends[k] = ends[k] * inverse
        for t in live:
            if t == top and low + group == tile_rows:
                continue
            for k in range(group):
                weight = columns[k][t]
                if t == top:
                    weight = jnp.where(row_of >= low + group, weight, 0.0)
                block[t] = block[t] - weight * rows[k]
                extra[t] = extra[t] - weight * ends[k]


def inverse_kernel(matrix_ref, out_ref, work_ref, tile_ref):
    size = matrix_ref.shape[0]
    work_ref[:, :size] = matrix_ref[...]
    row_of = lax.broadcasted_iota(jnp.int32, (size, size), 0)
    lane_of = lax.broadcasted_iota(jnp.int32, (size, size), 1)
    work_ref[:, size:] = jnp.where(row_of == lane_of, 1.0, 0.0)

    def step(index, carry):
        start = pl.multiple_of(index * lanes, lanes)

        def read_tile(t):
            return work_ref[pl.ds(start + t * tile_rows, tile_rows), pl.ds(start, lanes)]

        def write_row(at, value):
            tile_ref[at : at + 1, :] = value

        invert_tile(read_tile, write_row)
        solved = jnp.dot(
            tile_ref[...],
            work_ref[pl.ds(start, lanes), :],
            precision=highest,
            preferred_element_type=jnp.float32,
        )
        out_ref[pl.ds(start, lanes), :] = solved[:, size:]
        below = lax.broadcasted_iota(jnp.int32, (lanes, size), 1) >= start + lanes
        left = jnp.where(below, solved[:, :size], 0.0)
        work_ref[...] -= jnp.dot(
            left.T, solved, precision=highest, preferred_element_type=jnp.float32
        )
        return carry

    lax.fori_loop(0, size // lanes, step, 0)


def inverse_factor(matrix):
    size = matrix.shape[0]
    return pl.pallas_call(
        inverse_kernel,
        out_shape=jax.ShapeDtypeStruct((size, size), jnp.float32),
        in_specs=[pl.BlockSpec(memory_space=pltpu.VMEM)],
        out_specs=pl.BlockSpec(memory_space=pltpu.VMEM),
        scratch_shapes=[
            pltpu.VMEM((size, 2 * size), jnp.float32),
            pltpu.VMEM((lanes, lanes), jnp.float32),
        ],
        compiler_params=pltpu.CompilerParams(vmem_limit_bytes=32 * 1024 * 1024),
    )(matrix)


def remote(src, dst, send, recv, axis, target):
    return pltpu.make_async_remote_copy(
        src_ref=src,
        dst_ref=dst,
        send_sem=send,
        recv_sem=recv,
        device_id={axis: target},
        device_id_type=pl.DeviceIdType.MESH,
    )


def greet(axis, targets):
    barrier = pltpu.get_barrier_semaphore()
    for target in targets:
        pl.semaphore_signal(
            barrier, inc=1, device_id={axis: target}, device_id_type=pl.DeviceIdType.MESH
        )
    pl.semaphore_wait(barrier, len(targets))


def gather_kernel(axis, count, parts, block_ref, out_ref, send_sem, recv_sem):
    me = lax.axis_index(axis)
    odd = me % 2
    place = (1 - odd) * (me // 2) + odd * (count - 1 - me // 2)

    def member(spot):
        spot = (spot + count) % count
        upper = spot // (count // 2)
        return (1 - upper) * (2 * spot) + upper * (2 * (count - 1 - spot) + 1)

    right, left = member(place + 1), member(place - 1)
    greet(axis, (left, right))
    copies = []
    for step in range(count - 1):
        for lane, (start, stop) in enumerate(parts):
            way = lane % 2
            part = pl.ds(start, stop - start)
            owner = member(place - step) if way == 0 else member(place + step)
            source = block_ref.at[:, part] if step == 0 else out_ref.at[owner, :, part]
            copy = remote(
                source,
                out_ref.at[owner, :, part],
                send_sem.at[lane, step],
                recv_sem.at[lane, step],
                axis,
                right if way == 0 else left,
            )
            if step > 0:
                copies[len(parts) * (step - 1) + lane].wait_recv()
            copy.start()
            copies.append(copy)
        if step == 0:
            out_ref[me] = block_ref[...]
    for copy in copies[-len(parts) :]:
        copy.wait_recv()
    for copy in copies:
        copy.wait_send()


def gather_rows(block, axis):
    count = lax.axis_size(axis)
    rows, columns = block.shape
    pieces = columns // lanes
    cuts = [pieces * at // ring_parts * lanes for at in range(ring_parts)] + [columns]
    parts = tuple(zip(cuts[:-1], cuts[1:]))
    vmem = pl.BlockSpec(memory_space=pltpu.VMEM)
    return pl.pallas_call(
        functools.partial(gather_kernel, axis, count, parts),
        out_shape=jax.ShapeDtypeStruct((count, rows, columns), block.dtype),
        in_specs=[vmem],
        out_specs=vmem,
        scratch_shapes=[
            pltpu.SemaphoreType.DMA((ring_parts, count - 1)),
            pltpu.SemaphoreType.DMA((ring_parts, count - 1)),
        ],
        compiler_params=pltpu.CompilerParams(
            collective_id=0, has_side_effects=True, vmem_limit_bytes=32 * 1024 * 1024
        ),
    )(block)


def sum_kernel(axis, count, part_ref, sides_ref, total_ref, all_ref, out_buf, in_buf, send_sem, recv_sem):
    me = lax.axis_index(axis)
    rounds = count.bit_length() - 1
    greet(axis, [(me + shift) % count for shift in range(1, count)])
    copies = []
    for level in range(rounds):
        bit = 1 << level
        partner = me + (1 - 2 * ((me // bit) % 2)) * bit
        source = part_ref if level == 0 else out_buf.at[level]
        copy = remote(
            source, in_buf.at[level], send_sem.at[level], recv_sem.at[level], axis, partner
        )
        copy.start()
        if level == 0:
            for shift in range(1, count):
                spot = rounds + shift - 1
                copies.append(
                    remote(
                        sides_ref,
                        all_ref.at[me],
                        send_sem.at[spot],
                        recv_sem.at[spot],
                        axis,
                        (me + shift) % count,
                    )
                )
                copies[-1].start()
            all_ref[me] = sides_ref[...]
        copy.wait()
        total = source[...].astype(jnp.float32) + in_buf[level].astype(jnp.float32)
        if level + 1 < rounds:
            out_buf[level + 1] = total.astype(out_buf.dtype)
        else:
            total_ref[...] = total
    for copy in copies:
        copy.wait()


def sum_parts(part, sides, axis):
    count = lax.axis_size(axis)
    rounds = count.bit_length() - 1
    copies = rounds + count - 1
    vmem = pl.BlockSpec(memory_space=pltpu.VMEM)
    return pl.pallas_call(
        functools.partial(sum_kernel, axis, count),
        out_shape=(
            jax.ShapeDtypeStruct(part.shape, jnp.float32),
            jax.ShapeDtypeStruct((count,) + sides.shape, sides.dtype),
        ),
        in_specs=[vmem, vmem],
        out_specs=(vmem, vmem),
        scratch_shapes=[
            pltpu.VMEM((rounds,) + part.shape, part.dtype),
            pltpu.VMEM((rounds,) + part.shape, part.dtype),
            pltpu.SemaphoreType.DMA((copies,)),
            pltpu.SemaphoreType.DMA((copies,)),
        ],
        compiler_params=pltpu.CompilerParams(
            collective_id=1, has_side_effects=True, vmem_limit_bytes=32 * 1024 * 1024
        ),
    )(part, sides)


def finish_kernel(
    axis, count, rows_ref, inverse_ref, reduced_ref, right_ref, panel_ref, rest_ref,
    panel_buf, update_buf, land_buf, send_sem, recv_sem
):
    me = lax.axis_index(axis)
    width = panel_ref.shape[2]
    greet(axis, [(me + shift) % count for shift in range(1, count)])
    copies = []

    def send(kind, source, target_ref):
        for shift in range(1, count):
            target = (me + shift) % count
            copy = remote(
                source.at[target],
                target_ref.at[me],
                send_sem.at[kind, shift - 1],
                recv_sem.at[kind, shift - 1],
                axis,
                target,
            )
            copy.start()
            copies.append(copy)
        target_ref[me] = source[me]

    solved = lax.dot_general(
        rows_ref[...],
        inverse_ref[...],
        (((1,), (1,)), ((), ())),
        precision=highest,
        preferred_element_type=jnp.float32,
    )
    for part in range(count):
        panel_buf[part] = solved[:, part * width : (part + 1) * width]
    send(0, panel_buf, panel_ref)
    update = jnp.dot(
        solved, reduced_ref[...], precision=highest, preferred_element_type=jnp.float32
    )
    for part in range(count):
        update_buf[part] = update[:, part * width : (part + 1) * width]
    send(1, update_buf, land_buf)
    for copy in copies:
        copy.wait()
    rest_ref[...] = right_ref[...].astype(jnp.float32) - land_buf[...]


def finish(rows, inverse, reduced, right, axis):
    count = lax.axis_size(axis)
    shape = (count, rows.shape[0], right.shape[1])
    vmem = pl.BlockSpec(memory_space=pltpu.VMEM)
    out = jax.ShapeDtypeStruct(shape, jnp.float32)
    panel, rest = pl.pallas_call(
        functools.partial(finish_kernel, axis, count),
        out_shape=(out, out),
        in_specs=[vmem] * 4,
        out_specs=(vmem, vmem),
        scratch_shapes=[pltpu.VMEM(shape, jnp.float32)] * 3
        + [pltpu.SemaphoreType.DMA((2, count - 1))] * 2,
        compiler_params=pltpu.CompilerParams(
            collective_id=2, has_side_effects=True, vmem_limit_bytes=32 * 1024 * 1024
        ),
    )(rows, inverse, reduced, right.reshape(shape))
    return panel.reshape(right.shape), rest.reshape(right.shape)


def shards(window_points, pivot_points, window_factor, pivot_factor, right_sides, pivot_sides):
    depth, width = pivot_factor.shape[1], pivot_sides.shape[1]
    padded = jnp.pad(pivot_sides, ((0, 0), (0, -width % lanes)))
    gathered = gather_rows(jnp.concatenate([pivot_factor, padded], axis=1), "row")
    gathered = gathered.reshape(-1, gathered.shape[2])
    pivots, pivot_block = gathered[:, :depth], gathered[:, depth : depth + width]
    contract = (((1,), (1,)), ((), ()))
    gram_part = lax.dot_general(pivots, pivots, contract, preferred_element_type=jnp.float32)
    count = pivots.shape[0]
    cov_diagonal = matern(pivot_points, pivot_points) + nugget_value * jnp.eye(
        count, dtype=jnp.float32
    )
    layers = lax.axis_size("layer")
    layer_index = lax.axis_index("layer")
    rows_here = window_factor.shape[0] // layers
    own_points = lax.dynamic_slice_in_dim(window_points, layer_index * rows_here, rows_here, 1)
    cov_rows = matern(own_points, pivot_points)
    gram_sum, all_parts = sum_parts(gram_part.astype(jnp.bfloat16), pivot_block, "layer")
    gathered, gram_sum = lax.optimization_barrier((gathered, gram_sum))
    partial_value = lax.dot_general(
        window_factor, gathered[:, :depth], contract, preferred_element_type=jnp.float32
    )
    schur_part = lax.psum_scatter(partial_value, "layer", scatter_dimension=0, tiled=True)
    all_sides = jnp.swapaxes(all_parts, 0, 1).reshape(count, layers * width)
    inverse = inverse_factor(cov_diagonal - gram_sum)
    reduced = jnp.dot(inverse, all_sides.astype(jnp.float32), precision=highest)
    return finish(cov_rows - schur_part, inverse, reduced, right_sides, "layer")


def solution(mesh):
    placed = (
        P(None, "row"),
        P(),
        P("row", "layer"),
        P("row", "layer"),
        P("row", "layer"),
        P("row", "layer"),
    )
    return jax.shard_map(
        shards,
        mesh=mesh,
        in_specs=placed,
        out_specs=(P("row", "layer"), P("row", "layer")),
        check_vma=False,
    )
```

```python
import functools

import jax
import jax.numpy as jnp
from jax import lax
from jax.experimental import pallas as pl
from jax.experimental.pallas import tpu as pltpu
from jax.sharding import PartitionSpec as P

nugget_value = 2.0
variance_value = 4.0
length_scale = 4.0


def matern(first_points, second_points):
    first_float = first_points.astype(jnp.float32)
    second_float = second_points.astype(jnp.float32)
    delta_x = first_float[0][:, None] - second_float[0][None, :]
    delta_y = first_float[1][:, None] - second_float[1][None, :]
    scaled = jnp.sqrt(delta_x * delta_x + delta_y * delta_y) * (jnp.sqrt(3.0) / length_scale)
    return variance_value * (1.0 + scaled) * jnp.exp(-scaled)


lanes = 128
tile_rows = 8
group = 8
ring_parts = 4
highest = lax.Precision.HIGHEST


def invert_tile(read_tile, write_row):
    shape = (tile_rows, lanes)
    count = lanes // tile_rows
    row_of = lax.broadcasted_iota(jnp.int32, shape, 0)
    lane_of = lax.broadcasted_iota(jnp.int32, shape, 1)
    block = [read_tile(t) for t in range(count)]
    extra = [jnp.where(row_of + t * tile_rows == lane_of, 1.0, 0.0) for t in range(count)]
    for first in range(0, lanes, group):
        top, low = first // tile_rows, first % tile_rows
        live = range(top, count)
        columns = [
            {t: jnp.broadcast_to(block[t][:, first + k : first + k + 1], shape) for t in live}
            for k in range(group)
        ]

        def spread(tile, k):
            return jnp.broadcast_to(tile[low + k : low + k + 1, :], shape)

        rows = [spread(block[top], k) for k in range(group)]
        ends = [spread(extra[top], k) for k in range(group)]
        for k in range(group):
            pivot = spread(columns[k][top], k)
            inverse = 1.0 / pivot
            write_row(first + k, (ends[k] * lax.rsqrt(pivot))[0:1, :])
            for m in range(k + 1, group):
                factor = spread(columns[k][top], m) * inverse
                rows[m] = rows[m] - factor * rows[k]
                ends[m] = ends[m] - factor * ends[k]
                for t in live:
                    columns[m][t] = columns[m][t] - columns[k][t] * factor
            rows[k] = rows[k] * inverse
            ends[k] = ends[k] * inverse
        for t in live:
            if t == top and low + group == tile_rows:
                continue
            for k in range(group):
                weight = columns[k][t]
                if t == top:
                    weight = jnp.where(row_of >= low + group, weight, 0.0)
                block[t] = block[t] - weight * rows[k]
                extra[t] = extra[t] - weight * ends[k]


def inverse_kernel(matrix_ref, out_ref, work_ref, tile_ref):
    size = matrix_ref.shape[0]
    work_ref[:, :size] = matrix_ref[...]
    row_of = lax.broadcasted_iota(jnp.int32, (size, size), 0)
    lane_of = lax.broadcasted_iota(jnp.int32, (size, size), 1)
    work_ref[:, size:] = jnp.where(row_of == lane_of, 1.0, 0.0)

    def step(index, carry):
        start = pl.multiple_of(index * lanes, lanes)

        def read_tile(t):
            return work_ref[pl.ds(start + t * tile_rows, tile_rows), pl.ds(start, lanes)]

        def write_row(at, value):
            tile_ref[at : at + 1, :] = value

        invert_tile(read_tile, write_row)
        solved = jnp.dot(
            tile_ref[...],
            work_ref[pl.ds(start, lanes), :],
            precision=highest,
            preferred_element_type=jnp.float32,
        )
        out_ref[pl.ds(start, lanes), :] = solved[:, size:]

        @pl.when(index < size // lanes - 1)
        def reduce_rest():
            below = lax.broadcasted_iota(jnp.int32, (lanes, size), 1) >= start + lanes
            left = jnp.where(below, solved[:, :size], 0.0)
            work_ref[...] -= jnp.dot(
                left.T, solved, precision=highest, preferred_element_type=jnp.float32
            )

        return carry

    lax.fori_loop(0, size // lanes, step, 0)


def inverse_factor(matrix):
    size = matrix.shape[0]
    return pl.pallas_call(
        inverse_kernel,
        out_shape=jax.ShapeDtypeStruct((size, size), jnp.float32),
        in_specs=[pl.BlockSpec(memory_space=pltpu.VMEM)],
        out_specs=pl.BlockSpec(memory_space=pltpu.VMEM),
        scratch_shapes=[
            pltpu.VMEM((size, 2 * size), jnp.float32),
            pltpu.VMEM((lanes, lanes), jnp.float32),
        ],
        compiler_params=pltpu.CompilerParams(vmem_limit_bytes=32 * 1024 * 1024),
    )(matrix)


def remote(src, dst, send, recv, axis, target):
    return pltpu.make_async_remote_copy(
        src_ref=src,
        dst_ref=dst,
        send_sem=send,
        recv_sem=recv,
        device_id={axis: target},
        device_id_type=pl.DeviceIdType.MESH,
    )


def greet(axis, targets):
    barrier = pltpu.get_barrier_semaphore()
    for target in targets:
        pl.semaphore_signal(
            barrier, inc=1, device_id={axis: target}, device_id_type=pl.DeviceIdType.MESH
        )
    pl.semaphore_wait(barrier, len(targets))


def gather_kernel(axis, count, parts, block_ref, out_ref, send_sem, recv_sem):
    me = lax.axis_index(axis)
    odd = me % 2
    place = (1 - odd) * (me // 2) + odd * (count - 1 - me // 2)

    def member(spot):
        spot = (spot + count) % count
        upper = spot // (count // 2)
        return (1 - upper) * (2 * spot) + upper * (2 * (count - 1 - spot) + 1)

    right, left = member(place + 1), member(place - 1)
    greet(axis, (left, right))
    copies = []
    for step in range(count - 1):
        for lane, (start, stop) in enumerate(parts):
            way = lane % 2
            part = pl.ds(start, stop - start)
            owner = member(place - step) if way == 0 else member(place + step)
            source = block_ref.at[:, part] if step == 0 else out_ref.at[owner, :, part]
            copy = remote(
                source,
                out_ref.at[owner, :, part],
                send_sem.at[lane, step],
                recv_sem.at[lane, step],
                axis,
                right if way == 0 else left,
            )
            if step > 0:
                copies[len(parts) * (step - 1) + lane].wait_recv()
            copy.start()
            copies.append(copy)
        if step == 0:
            out_ref[me] = block_ref[...]
    for copy in copies[-len(parts) :]:
        copy.wait_recv()
    for copy in copies:
        copy.wait_send()


def gather_rows(block, axis):
    count = lax.axis_size(axis)
    rows, columns = block.shape
    pieces = columns // lanes
    cuts = [pieces * at // ring_parts * lanes for at in range(ring_parts)] + [columns]
    parts = tuple(zip(cuts[:-1], cuts[1:]))
    vmem = pl.BlockSpec(memory_space=pltpu.VMEM)
    return pl.pallas_call(
        functools.partial(gather_kernel, axis, count, parts),
        out_shape=jax.ShapeDtypeStruct((count, rows, columns), block.dtype),
        in_specs=[vmem],
        out_specs=vmem,
        scratch_shapes=[
            pltpu.SemaphoreType.DMA((ring_parts, count - 1)),
            pltpu.SemaphoreType.DMA((ring_parts, count - 1)),
        ],
        compiler_params=pltpu.CompilerParams(
            collective_id=0, has_side_effects=True, vmem_limit_bytes=32 * 1024 * 1024
        ),
    )(block)


def sum_kernel(axis, count, part_ref, sides_ref, total_ref, all_ref, out_buf, in_buf, send_sem, recv_sem):
    me = lax.axis_index(axis)
    rounds = count.bit_length() - 1
    greet(axis, [(me + shift) % count for shift in range(1, count)])
    copies = []
    for level in range(rounds):
        bit = 1 << level
        partner = me + (1 - 2 * ((me // bit) % 2)) * bit
        source = part_ref if level == 0 else out_buf.at[level]
        copy = remote(
            source, in_buf.at[level], send_sem.at[level], recv_sem.at[level], axis, partner
        )
        copy.start()
        if level == 0:
            for shift in range(1, count):
                spot = rounds + shift - 1
                copies.append(
                    remote(
                        sides_ref,
                        all_ref.at[me],
                        send_sem.at[spot],
                        recv_sem.at[spot],
                        axis,
                        (me + shift) % count,
                    )
                )
                copies[-1].start()
            all_ref[me] = sides_ref[...]
        copy.wait()
        total = source[...].astype(jnp.float32) + in_buf[level].astype(jnp.float32)
        if level + 1 < rounds:
            out_buf[level + 1] = total.astype(out_buf.dtype)
        else:
            total_ref[...] = total
    for copy in copies:
        copy.wait()


def sum_parts(part, sides, axis):
    count = lax.axis_size(axis)
    rounds = count.bit_length() - 1
    copies = rounds + count - 1
    vmem = pl.BlockSpec(memory_space=pltpu.VMEM)
    return pl.pallas_call(
        functools.partial(sum_kernel, axis, count),
        out_shape=(
            jax.ShapeDtypeStruct(part.shape, jnp.float32),
            jax.ShapeDtypeStruct((count,) + sides.shape, sides.dtype),
        ),
        in_specs=[vmem, vmem],
        out_specs=(vmem, vmem),
        scratch_shapes=[
            pltpu.VMEM((rounds,) + part.shape, part.dtype),
            pltpu.VMEM((rounds,) + part.shape, part.dtype),
            pltpu.SemaphoreType.DMA((copies,)),
            pltpu.SemaphoreType.DMA((copies,)),
        ],
        compiler_params=pltpu.CompilerParams(
            collective_id=1, has_side_effects=True, vmem_limit_bytes=32 * 1024 * 1024
        ),
    )(part, sides)


def finish_kernel(
    axis, count, rows_ref, inverse_ref, reduced_ref, right_ref, panel_ref, rest_ref,
    panel_buf, update_buf, land_buf, send_sem, recv_sem
):
    me = lax.axis_index(axis)
    width = panel_ref.shape[2]
    greet(axis, [(me + shift) % count for shift in range(1, count)])
    copies = []

    def send(kind, source, target_ref):
        for shift in range(1, count):
            target = (me + shift) % count
            copy = remote(
                source.at[target],
                target_ref.at[me],
                send_sem.at[kind, shift - 1],
                recv_sem.at[kind, shift - 1],
                axis,
                target,
            )
            copy.start()
            copies.append(copy)
        target_ref[me] = source[me]

    solved = lax.dot_general(
        rows_ref[...],
        inverse_ref[...],
        (((1,), (1,)), ((), ())),
        precision=highest,
        preferred_element_type=jnp.float32,
    )
    for part in range(count):
        panel_buf[part] = solved[:, part * width : (part + 1) * width]
    send(0, panel_buf, panel_ref)
    update = jnp.dot(
        solved, reduced_ref[...], precision=highest, preferred_element_type=jnp.float32
    )
    for part in range(count):
        update_buf[part] = update[:, part * width : (part + 1) * width]
    send(1, update_buf, land_buf)
    for copy in copies:
        copy.wait()
    rest_ref[...] = right_ref[...].astype(jnp.float32) - land_buf[...]


def finish(rows, inverse, reduced, right, axis):
    count = lax.axis_size(axis)
    shape = (count, rows.shape[0], right.shape[1])
    vmem = pl.BlockSpec(memory_space=pltpu.VMEM)
    out = jax.ShapeDtypeStruct(shape, jnp.float32)
    panel, rest = pl.pallas_call(
        functools.partial(finish_kernel, axis, count),
        out_shape=(out, out),
        in_specs=[vmem] * 4,
        out_specs=(vmem, vmem),
        scratch_shapes=[pltpu.VMEM(shape, jnp.float32)] * 3
        + [pltpu.SemaphoreType.DMA((2, count - 1))] * 2,
        compiler_params=pltpu.CompilerParams(
            collective_id=2, has_side_effects=True, vmem_limit_bytes=32 * 1024 * 1024
        ),
    )(rows, inverse, reduced, right.reshape(shape))
    return panel.reshape(right.shape), rest.reshape(right.shape)


def shards(window_points, pivot_points, window_factor, pivot_factor, right_sides, pivot_sides):
    depth, width = pivot_factor.shape[1], pivot_sides.shape[1]
    padded = jnp.pad(pivot_sides, ((0, 0), (0, -width % lanes)))
    gathered = gather_rows(jnp.concatenate([pivot_factor, padded], axis=1), "row")
    gathered = gathered.reshape(-1, gathered.shape[2])
    pivots, pivot_block = gathered[:, :depth], gathered[:, depth : depth + width]
    contract = (((1,), (1,)), ((), ()))
    gram_part = lax.dot_general(pivots, pivots, contract, preferred_element_type=jnp.float32)
    count = pivots.shape[0]
    cov_diagonal = matern(pivot_points, pivot_points) + nugget_value * jnp.eye(
        count, dtype=jnp.float32
    )
    layers = lax.axis_size("layer")
    layer_index = lax.axis_index("layer")
    rows_here = window_factor.shape[0] // layers
    own_points = lax.dynamic_slice_in_dim(window_points, layer_index * rows_here, rows_here, 1)
    cov_rows = matern(own_points, pivot_points)
    gram_sum, all_parts = sum_parts(gram_part.astype(jnp.bfloat16), pivot_block, "layer")
    gathered, gram_sum = lax.optimization_barrier((gathered, gram_sum))
    partial_value = lax.dot_general(
        window_factor, gathered[:, :depth], contract, preferred_element_type=jnp.float32
    )
    schur_part = lax.psum_scatter(partial_value, "layer", scatter_dimension=0, tiled=True)
    all_sides = jnp.swapaxes(all_parts, 0, 1).reshape(count, layers * width)
    inverse = inverse_factor(cov_diagonal - gram_sum)
    reduced = jnp.dot(inverse, all_sides.astype(jnp.float32), precision=highest)
    return finish(cov_rows - schur_part, inverse, reduced, right_sides, "layer")


def solution(mesh):
    placed = (
        P(None, "row"),
        P(),
        P("row", "layer"),
        P("row", "layer"),
        P("row", "layer"),
        P("row", "layer"),
    )
    return jax.shard_map(
        shards,
        mesh=mesh,
        in_specs=placed,
        out_specs=(P("row", "layer"), P("row", "layer")),
        check_vma=False,
    )
```
